32 devices in a mesh: row: 8 (over y, x, core), col: 4 (over z).
Axes of the slice: x: 2, y: 2, z: 4, core: 2. Of those that a mesh axis runs over, the one named last changes fastest.
Arguments:
- panel_cols: bfloat16 [48, 2048, 512], P('col', 'row'), may hold values from -6 to 6
- inverses: bfloat16 [2, 256, 256], replicated, as said below
- trailing: bfloat16 [48, 2048, 1024], P(None, 'row', 'col'), may hold values from -6 to 6
Outputs:
- updated: bfloat16 [48, 2048, 1024], P(None, 'row', 'col')
The draws below stay inside these ranges and needn't reach their ends.
Inputs may be any that keep to these rules, and one draw needn't show every extreme that they name: `inverses`: each of the two 256 x 256 matrices is lower triangular with a positive diagonal.
All inputs are finite; a program needn't handle non-finite values.
Results may differ from the reference program's by a relative error of at most 0.0063.
Values may be sent and summed in bfloat16 or wider, within the bound.
No kernel may reach another device: no remote copies, remote signals or barrier semaphores. Data moves between devices by JAX's collectives and lax.ppermute only.
A program may use at most 128 MiB of HBM per device.

```python
import jax
import jax.numpy as jnp
from jax import lax

TILE = 256
TR_DEV = 48
TRAIL = 1024
N_ROW = 8
N_COL = 4


def draw_inverses(key, part):
    first_key, second_key = jax.random.split(jax.random.fold_in(key, 7))
    below = (jnp.arange(TILE)[:, None] > jnp.arange(TILE)[None, :]).astype(jnp.float32)
    identity = jnp.eye(TILE, dtype=jnp.float32)
    lower_part = jax.random.normal(first_key, (2, TILE, TILE), jnp.float32) / 64.0
    diag_vals = jax.random.uniform(second_key, (2, TILE, 1), jnp.float32, 0.2, 0.35)
    matrix = lower_part * below[None] + diag_vals * identity[None]
    return matrix.astype(jnp.bfloat16)


def shard_levels(own_key, extent, cuts, smallest, largest):
    loudness = 1.0
    for position, shards_of in cuts:
        steps = jax.random.uniform(jax.random.fold_in(jax.random.fold_in(own_key, 6), position), (shards_of,), jnp.float32, smallest / len(cuts), largest / len(cuts))
        loudness = loudness * jnp.repeat(jnp.exp(steps), extent[position] // shards_of).reshape((-1,) + (1,) * (len(extent) - 1 - position))
    return loudness


def noise(own_key, extent, width, limit, cuts=(), kind=jnp.bfloat16):
    gain = shard_levels(own_key, extent, cuts, -0.22, 0.18) if cuts else 1.0
    values = jax.random.normal(own_key, extent, jnp.float32) * width * gain
    return jnp.minimum(jnp.maximum(values, -limit), limit).astype(kind)


def setup_inputs(seed: int = 0) -> dict:
    arg_keys = jax.random.split(jax.random.key(seed), 4)
    panel_cols = noise(arg_keys[0], (TR_DEV, N_ROW * TILE, 2 * TILE), 1.0, 6.0, ((0, 4), (1, 8)))
    inverses = draw_inverses(jax.random.fold_in(arg_keys[3], 71), 0)
    trailing = noise(arg_keys[2], (TR_DEV, N_ROW * TILE, TRAIL), 1.0, 6.0, ((1, 8), (2, 4)))
    return {"panel_cols": panel_cols, "inverses": inverses, "trailing": trailing}


def reference(panel_cols, inverses, trailing):
    flat_panel = panel_cols.reshape(-1, 2 * TILE)
    left_factor = jnp.dot(flat_panel[:, :TILE], inverses[0].T, preferred_element_type=jnp.float32).astype(jnp.bfloat16)
    couple_tile = left_factor[TILE:2 * TILE]
    reduced = (flat_panel[:, TILE:].astype(jnp.float32) - jnp.dot(left_factor, couple_tile.T, preferred_element_type=jnp.float32)).astype(jnp.bfloat16)
    right_factor = jnp.dot(reduced, inverses[1].T, preferred_element_type=jnp.float32).astype(jnp.bfloat16)
    factored = jnp.concatenate([left_factor, right_factor], axis=1)
    key_rows = factored[2 * TILE:(N_COL + 2) * TILE].reshape(N_COL, TILE, 2 * TILE)
    columns = jnp.moveaxis(trailing.reshape(-1, N_COL, TILE), 1, 0)

    def update_column(column_pair):
        column_block, key_tile = column_pair
        return (column_block.astype(jnp.float32) - jnp.dot(factored, key_tile.T, preferred_element_type=jnp.float32)).astype(jnp.bfloat16)

    result = lax.map(update_column, (columns, key_rows))
    return jnp.moveaxis(result, 0, 1).reshape(trailing.shape)
```

```python
import functools

import jax
import jax.numpy as jnp
from jax import lax
from jax.experimental import pallas as pl
from jax.experimental.pallas import tpu as pltpu
from jax.sharding import PartitionSpec as P


def dot_nt(left, right):
    return jnp.einsum("tak,bk->tab", left, right, preferred_element_type=jnp.float32)


def factor(panel, inverses, couple_tile):
    size = couple_tile.shape[0]
    left = dot_nt(panel[:, :, :size], inverses[0]).astype(jnp.bfloat16)
    reduced = (
        panel[:, :, size:].astype(jnp.float32) - dot_nt(left, couple_tile)
    ).astype(jnp.bfloat16)
    right = dot_nt(reduced, inverses[1]).astype(jnp.bfloat16)
    return jnp.concatenate([left, right], axis=2)


def product(factored, key_tile):
    return dot_nt(factored, key_tile).astype(jnp.bfloat16)


def pick(choices, index):
    return lax.dynamic_index_in_dim(choices, index, 0, keepdims=False)


def update_body(place, held, trailing, first, second, out):
    del held
    total = trailing[...].astype(jnp.float32)

    @pl.when(place[1] == 0)
    def _():
        out[...] = (total - first[...].astype(jnp.float32)).astype(out.dtype)

    @pl.when(place[1] != 0)
    def _():
        out[...] = (total - second[...].astype(jnp.float32)).astype(out.dtype)


def update(held, trailing, first, second, start, use_second):
    tiles, size, width = first.shape
    step = 2 if tiles % 2 == 0 else 1
    block = (step, size, width)
    place = jnp.stack([start // step, use_second]).astype(jnp.int32)
    body = update_body
    args = [trailing, first, second]
    in_specs = [
        pl.BlockSpec(block, lambda t, p: (p[0] + t, 0, 0)),
        pl.BlockSpec(block, lambda t, p: (jnp.where(p[1] == 0, t, 0), 0, 0)),
        pl.BlockSpec(block, lambda t, p: (jnp.where(p[1] == 0, 0, t), 0, 0)),
    ]
    aliases = {}
    if held is None:
        body = lambda place, *refs: update_body(place, None, *refs)
    else:
        args = [held] + args
        in_specs = [pl.BlockSpec(memory_space=pl.ANY)] + in_specs
        aliases = {1: 0}
    return pl.pallas_call(
        body,
        out_shape=jax.ShapeDtypeStruct(trailing.shape, trailing.dtype),
        grid_spec=pltpu.PrefetchScalarGridSpec(
            num_scalar_prefetch=1,
            grid=(tiles // step,),
            in_specs=in_specs,
            out_specs=pl.BlockSpec(block, lambda t, p: (p[0] + t, 0, 0)),
        ),
        input_output_aliases=aliases,
        cost_estimate=pl.CostEstimate(
            flops=first.size, bytes_accessed=6 * first.size, transcendentals=0
        ),
    )(place, *args)


def key_tiles(head, rows, cols, first_tile):
    row_index = lax.axis_index("row")
    col_index = lax.axis_index("col")
    wanted = sorted({tile % rows for tile in range(first_tile, cols + 2)})
    span = cols // 2
    while span:
        pairs = [
            (r * cols + c, r * cols + c + span)
            for r in wanted
            for c in range(0, cols, 2 * span)
        ]
        arrived = lax.ppermute(head, ("row", "col"), pairs)
        head = jnp.where(col_index % (2 * span) == span, arrived, head)
        span //= 2
    same = [head]
    for offset in range(2, rows, 2):
        same.append(lax.ppermute(head, "row", [(r, r ^ offset) for r in wanted]))
    same = jnp.stack(same)
    other = lax.ppermute(same, "row", [(r, r ^ 1) for r in range(rows)])
    heads = jnp.concatenate([same, other])
    tiles = []
    for tile in range(first_tile, cols + 2):
        offset = row_index ^ (tile % rows)
        tiles.append(pick(heads, offset // 2 + (offset % 2) * (rows // 2))[tile // rows])
    return tiles


def shards(panel_cols, inverses, trailing):
    tiles, size, _ = panel_cols.shape
    rows = lax.axis_size("row")
    cols = lax.axis_size("col")
    col_index = lax.axis_index("col")
    low, high = cols // 2 - 1, cols // 2
    in_low = col_index <= low
    inner = jnp.where(in_low, low, high)
    parts = 3 if tiles % 3 == 0 else 1
    part = tiles // parts

    raw = [
        lax.ppermute(panel_cols[i * part:(i + 1) * part], "col", [(low, high), (high, low)])
        for i in range(parts)
    ]

    head_tiles = (cols + 1) // rows + 1
    raw_keys = key_tiles(panel_cols[:head_tiles], rows, cols, 1)
    couple_tile = dot_nt(raw_keys[0][None, :, :size], inverses[0]).astype(jnp.bfloat16)[0]
    keys = factor(jnp.stack(raw_keys[1:]), inverses, couple_tile)

    factored = factor(panel_cols, inverses, couple_tile)
    arrived = {}
    for offset in range(1, cols):
        pairs = [
            (c, (c + offset) % cols)
            for c in range(cols)
            if not (c == low and (c + offset) % cols > low)
            and not (c == high and (c + offset) % cols < high)
        ]
        piece = product(factored, pick(keys, (col_index + offset) % cols))
        arrived[offset] = lax.ppermute(piece, "col", pairs)

    own = product(factored, pick(keys, col_index))
    out = update(None, trailing, own, own, col_index * tiles, jnp.int32(0))

    special = jnp.where(in_low, high, low)
    for i in range(parts):
        crossed = factor(raw[i], inverses, couple_tile)
        mine = product(crossed, pick(keys, col_index))
        handed = jnp.zeros_like(mine)
        for k in range(1, cols // 2):
            target = jnp.clip(jnp.where(in_low, col_index - k, col_index + k), 0, cols - 1)
            piece = product(crossed, pick(keys, target))
            got = lax.ppermute(piece, "col", [(high, high + k), (low, low - k)])
            handed = got if cols == 4 else jnp.where(jnp.abs(col_index - inner) == k, got, handed)
        out = update(
            out, trailing, mine, handed, special * tiles + i * part, (col_index != inner).astype(jnp.int32)
        )

    for offset in range(1, cols):
        source = (col_index - offset) % cols
        skip = source == special
        out = update(
            out,
            trailing,
            arrived[offset],
            own,
            jnp.where(skip, col_index, source) * tiles,
            skip.astype(jnp.int32),
        )
    return out


def solution(mesh):
    in_specs = (P("col", "row", None), P(), P(None, "row", "col"))
    out_specs = P(None, "row", "col")
    return jax.shard_map(shards, mesh=mesh, in_specs=in_specs, out_specs=out_specs, check_vma=False)
```

```python
import functools

import jax
import jax.numpy as jnp
from jax import lax
from jax.experimental import pallas as pl
from jax.experimental.pallas import tpu as pltpu
from jax.sharding import PartitionSpec as P

VMEM_LIMIT = 40 * 1024 * 1024
BF16 = jnp.bfloat16


def dot(left, right):
    return jnp.dot(left, right, preferred_element_type=jnp.float32)


def factor_rows(rows, inverses_t, couple_t):
    size = couple_t.shape[0]
    left = dot(rows[:, :size], inverses_t[0]).astype(BF16)
    reduced = (rows[:, size:].astype(jnp.float32) - dot(left, couple_t)).astype(BF16)
    right = dot(reduced, inverses_t[1]).astype(BF16)
    return left, right


def times_key(left, right, key_t):
    size = left.shape[1]
    return dot(left, key_t[:size]) + dot(right, key_t[size:])


def special_source(col, cols):
    return jnp.where(col < cols // 2, cols // 2, cols // 2 - 1)


def keys_body(rows, info, same, other, inverses_t, couple_t, keys_t):
    size = couple_t.shape[0]

    def raw(tile):
        offset = info[0] ^ (tile % rows)
        index, place = offset // 2, tile // rows
        return jnp.where(offset % 2 == 0, same[index, place], other[index, place])

    couple = dot(raw(1)[:, :size], inverses_t[0]).astype(BF16)
    couple_t[...] = couple.astype(jnp.float32).T.astype(BF16)
    for j in range(keys_t.shape[0]):
        left, right = factor_rows(raw(j + 2), inverses_t, couple_t[...])
        keys_t[j, :size] = left.astype(jnp.float32).T.astype(BF16)
        keys_t[j, size:] = right.astype(jnp.float32).T.astype(BF16)


def make_keys(info, same, other, inverses_t, rows, cols):
    size, width = same.shape[2:]
    vmem = pl.BlockSpec(memory_space=pltpu.VMEM)
    return pl.pallas_call(
        functools.partial(keys_body, rows),
        in_specs=[pl.BlockSpec(memory_space=pltpu.SMEM), vmem, vmem, vmem],
        out_specs=[vmem, vmem],
        out_shape=[
            jax.ShapeDtypeStruct((size, size), BF16),
            jax.ShapeDtypeStruct((cols, width, size), BF16),
        ],
        compiler_params=pltpu.CompilerParams(vmem_limit_bytes=VMEM_LIMIT),
        cost_estimate=pl.CostEstimate(
            flops=8 * cols * size**3, bytes_accessed=8 * cols * width * size, transcendentals=0
        ),
    )(info, same, other, inverses_t)


def own_body(cols, info, panel, inverses_t, couple_t, keys_t, trailing, out, *pieces):
    part, size, width = panel.shape
    left, right = factor_rows(panel[...].reshape(part * size, width), inverses_t, couple_t[...])
    for offset in range(cols):
        total = times_key(left, right, keys_t[info[1] ^ offset]).reshape(part, size, size)
        if offset == 0:
            out[...] = (trailing[...].astype(jnp.float32) - total).astype(BF16)
        else:
            pieces[offset - 1][...] = total.astype(BF16)


def own_tiles(info, panel, inverses_t, couple_t, keys_t, trailing, part, near_raw, cols):
    tiles, size, width = panel.shape
    parts = tiles // part
    block = (part, size, size)

    def whole(array):
        return pl.BlockSpec(array.shape, lambda t, p: (0,) * array.ndim)

    mine = pl.BlockSpec(block, lambda t, p: (p[1] * parts + t, 0, 0))
    near = pl.BlockSpec(block, lambda t, p: (jnp.maximum(t - near_raw, 0), 0, 0))
    far = pl.BlockSpec(block, lambda t, p: (t, 0, 0))
    piece = jax.ShapeDtypeStruct((tiles, size, size), BF16)
    near_piece = jax.ShapeDtypeStruct((tiles - near_raw * part, size, size), BF16)
    return pl.pallas_call(
        functools.partial(own_body, cols),
        grid_spec=pltpu.PrefetchScalarGridSpec(
            num_scalar_prefetch=1,
            grid=(parts,),
            in_specs=[
                pl.BlockSpec((part, size, width), lambda t, p: (t, 0, 0)),
                whole(inverses_t),
                whole(couple_t),
                whole(keys_t),
                mine,
            ],
            out_specs=[mine, near] + [far] * (cols - 2),
        ),
        out_shape=[jax.ShapeDtypeStruct(trailing.shape, BF16), near_piece]
        + [piece] * (cols - 2),
        compiler_params=pltpu.CompilerParams(vmem_limit_bytes=VMEM_LIMIT),
        cost_estimate=pl.CostEstimate(
            flops=2 * tiles * size**3 * (3 + 2 * cols),
            bytes_accessed=2 * tiles * size * size * (3 + cols),
            transcendentals=0,
        ),
    )(info, panel, inverses_t, couple_t, keys_t, trailing)


def near_body(info, held, raw, inverses_t, couple_t, keys_t, trailing, out):
    del held
    part, size, width = raw.shape
    left, right = factor_rows(raw[...].reshape(part * size, width), inverses_t, couple_t[...])
    total = times_key(left, right, keys_t[info[1]]).reshape(part, size, size)
    out[...] = (trailing[...].astype(jnp.float32) - total).astype(BF16)


def near_tiles(info, held, raw, index, inverses_t, couple_t, keys_t, trailing, parts):
    part, size, width = raw.shape

    def whole(array):
        return pl.BlockSpec(array.shape, lambda t, p: (0,) * array.ndim)

    place = pl.BlockSpec((part, size, size), lambda t, p: ((p[1] ^ 1) * parts + index, 0, 0))
    return pl.pallas_call(
        near_body,
        grid_spec=pltpu.PrefetchScalarGridSpec(
            num_scalar_prefetch=1,
            grid=(1,),
            in_specs=[
                pl.BlockSpec(memory_space=pl.ANY),
                whole(raw),
                whole(inverses_t),
                whole(couple_t),
                whole(keys_t),
                place,
            ],
            out_specs=place,
        ),
        out_shape=jax.ShapeDtypeStruct(trailing.shape, BF16),
        input_output_aliases={1: 0},
        compiler_params=pltpu.CompilerParams(vmem_limit_bytes=VMEM_LIMIT),
        cost_estimate=pl.CostEstimate(
            flops=10 * part * size**3, bytes_accessed=8 * part * size * size, transcendentals=0
        ),
    )(info, held, raw, inverses_t, couple_t, keys_t, trailing)


def crossed_body(cols, info, held, raw, inverses_t, couple_t, keys_t, kept, *pieces):
    del held, kept
    part, size, width = raw.shape
    left, right = factor_rows(raw[...].reshape(part * size, width), inverses_t, couple_t[...])
    col = info[1]
    for k in range(cols // 2):
        target = jnp.clip(jnp.where(col < cols // 2, col - k, col + k), 0, cols - 1)
        total = times_key(left, right, keys_t[target])
        pieces[k][...] = total.reshape(part, size, size).astype(BF16)


def crossed_tiles(info, held, raw, inverses_t, couple_t, keys_t, cols):
    part, size, width = raw.shape
    vmem = pl.BlockSpec(memory_space=pltpu.VMEM)
    anywhere = pl.BlockSpec(memory_space=pl.ANY)
    pieces = [jax.ShapeDtypeStruct((part, size, size), BF16)] * (cols // 2)
    out = pl.pallas_call(
        functools.partial(crossed_body, cols),
        in_specs=[pl.BlockSpec(memory_space=pltpu.SMEM), anywhere, vmem, vmem, vmem, vmem],
        out_specs=[anywhere] + [vmem] * (cols // 2),
        out_shape=[jax.ShapeDtypeStruct(held.shape, BF16)] + pieces,
        input_output_aliases={1: 0},
        compiler_params=pltpu.CompilerParams(vmem_limit_bytes=VMEM_LIMIT),
        cost_estimate=pl.CostEstimate(
            flops=2 * part * size**3 * (3 + cols), bytes_accessed=8 * part * size * size, transcendentals=0
        ),
    )(info, held, raw, inverses_t, couple_t, keys_t)
    return out[0], out[1:]


def update_body(use_second, info, held, trailing, first, second, out):
    del held
    flag = use_second(info[1])

    @pl.when(jnp.logical_not(flag))
    def _():
        out[...] = (trailing[...].astype(jnp.float32) - first[...].astype(jnp.float32)).astype(BF16)

    @pl.when(flag)
    def _():
        out[...] = (trailing[...].astype(jnp.float32) - second[...].astype(jnp.float32)).astype(BF16)


def update(info, held, trailing, first, second, part, start, use_second):
    tiles, size, width = first.shape
    block = (part, size, width)
    place = pl.BlockSpec(block, lambda t, p: (start(p[1]) + t, 0, 0))
    return pl.pallas_call(
        functools.partial(update_body, use_second),
        grid_spec=pltpu.PrefetchScalarGridSpec(
            num_scalar_prefetch=1,
            grid=(tiles // part,),
            in_specs=[
                pl.BlockSpec(memory_space=pl.ANY),
                place,
                pl.BlockSpec(block, lambda t, p: (jnp.where(use_second(p[1]), 0, t), 0, 0)),
                pl.BlockSpec(block, lambda t, p: (jnp.where(use_second(p[1]), t, 0), 0, 0)),
            ],
            out_specs=place,
        ),
        out_shape=jax.ShapeDtypeStruct(trailing.shape, trailing.dtype),
        input_output_aliases={1: 0},
        compiler_params=pltpu.CompilerParams(vmem_limit_bytes=VMEM_LIMIT),
        cost_estimate=pl.CostEstimate(
            flops=first.size, bytes_accessed=6 * first.size, transcendentals=0
        ),
    )(info, held, trailing, first, second)


def spread_heads(head, rows, cols):
    wanted = sorted({tile % rows for tile in range(1, cols + 2)})
    col_index = lax.axis_index("col")
    span = cols // 2
    while span:
        pairs = [
            (r * cols + c, r * cols + c + span) for r in wanted for c in range(0, cols, 2 * span)
        ]
        arrived = lax.ppermute(head, ("row", "col"), pairs)
        head = jnp.where(col_index % (2 * span) == span, arrived, head)
        span //= 2
    same = [head]
    for offset in range(2, rows, 2):
        same.append(lax.ppermute(head, "row", [(r, r ^ offset) for r in wanted]))
    same = jnp.stack(same)
    return same, lax.ppermute(same, "row", [(r, r ^ 1) for r in range(rows)])


def shards(panel_cols, inverses, trailing):
    tiles = panel_cols.shape[0]
    rows = lax.axis_size("row")
    cols = lax.axis_size("col")
    low, high = cols // 2 - 1, cols // 2
    parts = 3 if tiles % 3 == 0 else 1
    part = tiles // parts
    near_raw = parts - 1
    info = jnp.stack([lax.axis_index("row"), lax.axis_index("col")]).astype(jnp.int32)
    inverses_t = jnp.swapaxes(inverses, 1, 2)

    chunks = [panel_cols[i * part:(i + 1) * part] for i in range(parts)]
    swap = [(low, high), (high, low)]
    beside = [(c, c ^ 1) for c in range(cols)]
    crossed = [lax.ppermute(chunk, "col", swap) for chunk in chunks]
    next_raw = [lax.ppermute(chunk, "col", beside) for chunk in chunks[:near_raw]]

    head_tiles = (cols + 1) // rows + 1
    same, other = spread_heads(panel_cols[:head_tiles], rows, cols)
    couple_t, keys_t = make_keys(info, same, other, inverses_t, rows, cols)
    small = (inverses_t, couple_t, keys_t)

    out, near, *far = own_tiles(info, panel_cols, *small, trailing, part, near_raw, cols)
    arrived = {1: lax.ppermute(near, "col", beside)}
    for offset in range(cols - 1, 1, -1):
        pairs = [
            (c, c ^ offset)
            for c in range(cols)
            if not (c == low and c ^ offset > low) and not (c == high and c ^ offset < high)
        ]
        arrived[offset] = lax.ppermute(far[offset - 2], "col", pairs)

    for i in range(near_raw):
        out = near_tiles(info, out, next_raw[i], i, *small, trailing, parts)

    outward = []
    col_index = lax.axis_index("col")
    for i in range(parts):
        out, (mine, *handed) = crossed_tiles(info, out, crossed[i], *small, cols)
        got = [
            lax.ppermute(handed[k], "col", [(high, high + k + 1), (low, low - k - 1)])
            for k in range(cols // 2 - 1)
        ]
        chosen = got[0]
        for k in range(1, len(got)):
            here = (col_index == high + k + 1) | (col_index == low - k - 1)
            chosen = jnp.where(here, got[k], chosen)
        outward.append((mine, chosen))

    never = lambda col: col < 0
    out = update(
        info, out, trailing, arrived[1], arrived[1], part,
        lambda col: (col ^ 1) * parts + near_raw, never,
    )

    def outer(col):
        return (col != low) & (col != high)

    for i, (mine, got) in enumerate(outward[:-1]):
        out = update(
            info, out, trailing, mine, got, part,
            lambda col, i=i: special_source(col, cols) * parts + i, outer,
        )
    for offset in range(2, cols - 1):
        def second(col, offset=offset):
            return (col ^ special_source(col, cols)) <= offset

        def source(col, offset=offset, second=second):
            return (col ^ jnp.where(second(col), offset + 1, offset)) * parts

        out = update(
            info, out, trailing, arrived[offset], arrived[offset + 1], part, source, second
        )
    mine, got = outward[-1]
    return update(
        info, out, trailing, mine, got, part,
        lambda col: special_source(col, cols) * parts + parts - 1, outer,
    )


def solution(mesh):
    in_specs = (P("col", "row", None), P(), P(None, "row", "col"))
    out_specs = P(None, "row", "col")
    return jax.shard_map(shards, mesh=mesh, in_specs=in_specs, out_specs=out_specs, check_vma=False)
```

```python
import functools

import jax
import jax.numpy as jnp
from jax import lax
from jax.experimental import pallas as pl
from jax.experimental.pallas import tpu as pltpu
from jax.sharding import PartitionSpec as P

VMEM_LIMIT = 40 * 1024 * 1024
BF16 = jnp.bfloat16
SMALL_COST = pl.CostEstimate(flops=1024, bytes_accessed=1024, transcendentals=0)


def dot(left, right):
    return jnp.dot(left, right, preferred_element_type=jnp.float32)


def factor_rows(rows, inverses_t, couple_t):
    size = couple_t.shape[0]
    left = dot(rows[:, :size], inverses_t[0]).astype(BF16)
    reduced = (rows[:, size:].astype(jnp.float32) - dot(left, couple_t)).astype(BF16)
    right = dot(reduced, inverses_t[1]).astype(BF16)
    return left, right


def times_key(left, right, key_t):
    size = left.shape[1]
    return dot(left, key_t[:size]) + dot(right, key_t[size:])


def special_source(col, cols):
    return jnp.where(col < cols // 2, cols // 2, cols // 2 - 1)


def keys_body(rows, info, same, other, inverses_t, couple_t, keys_t):
    size = couple_t.shape[0]

    def raw(tile):
        offset = info[0] ^ (tile % rows)
        index, place = offset // 2, tile // rows
        return jnp.where(offset % 2 == 0, same[index, place], other[index, place])

    couple = dot(raw(1)[:, :size], inverses_t[0]).astype(BF16)
    couple_t[...] = couple.astype(jnp.float32).T.astype(BF16)
    for j in range(keys_t.shape[0]):
        left, right = factor_rows(raw(j + 2), inverses_t, couple_t[...])
        keys_t[j, :size] = left.astype(jnp.float32).T.astype(BF16)
        keys_t[j, size:] = right.astype(jnp.float32).T.astype(BF16)


def make_keys(info, same, other, inverses_t, rows, cols):
    size, width = same.shape[2:]
    vmem = pl.BlockSpec(memory_space=pltpu.VMEM)
    return pl.pallas_call(
        functools.partial(keys_body, rows),
        in_specs=[pl.BlockSpec(memory_space=pltpu.SMEM), vmem, vmem, vmem],
        out_specs=[vmem, vmem],
        out_shape=[
            jax.ShapeDtypeStruct((size, size), BF16),
            jax.ShapeDtypeStruct((cols, width, size), BF16),
        ],
        compiler_params=pltpu.CompilerParams(vmem_limit_bytes=VMEM_LIMIT),
        cost_estimate=SMALL_COST,
    )(info, same, other, inverses_t)


def whole(array):
    return pl.BlockSpec(array.shape, lambda t, p: (0,) * array.ndim)


def own_body(cols, info, panel, inverses_t, couple_t, keys_t, trailing, out, *pieces):
    part, size, width = panel.shape
    left, right = factor_rows(panel[...].reshape(part * size, width), inverses_t, couple_t[...])
    total = times_key(left, right, keys_t[info[1]]).reshape(part, size, size)
    out[...] = (trailing[...].astype(jnp.float32) - total).astype(BF16)
    for offset in range(2, cols):
        total = times_key(left, right, keys_t[info[1] ^ offset]).reshape(part, size, size)
        pieces[offset - 2][...] = total.astype(BF16)


def own_tiles(info, panel, inverses_t, couple_t, keys_t, trailing, part, cols):
    tiles, size, width = panel.shape
    parts = tiles // part
    block = (part, size, size)
    mine = pl.BlockSpec(block, lambda t, p: (p[1] * parts + t, 0, 0))
    far = pl.BlockSpec(block, lambda t, p: (t, 0, 0))
    piece = jax.ShapeDtypeStruct((tiles, size, size), BF16)
    return pl.pallas_call(
        functools.partial(own_body, cols),
        grid_spec=pltpu.PrefetchScalarGridSpec(
            num_scalar_prefetch=1,
            grid=(parts,),
            in_specs=[
                pl.BlockSpec((part, size, width), lambda t, p: (t, 0, 0)),
                whole(inverses_t),
                whole(couple_t),
                whole(keys_t),
                mine,
            ],
            out_specs=[mine] + [far] * (cols - 2),
        ),
        out_shape=[jax.ShapeDtypeStruct(trailing.shape, BF16)] + [piece] * (cols - 2),
        compiler_params=pltpu.CompilerParams(vmem_limit_bytes=VMEM_LIMIT),
        cost_estimate=SMALL_COST,
    )(info, panel, inverses_t, couple_t, keys_t, trailing)


def near_body(info, held, after, raw, inverses_t, couple_t, keys_t, trailing, out):
    del held, after
    part, size, width = raw.shape
    left, right = factor_rows(raw[...].reshape(part * size, width), inverses_t, couple_t[...])
    total = times_key(left, right, keys_t[info[1]]).reshape(part, size, size)
    out[...] = (trailing[...].astype(jnp.float32) - total).astype(BF16)


def near_tiles(info, held, after, raw, inverses_t, couple_t, keys_t, trailing, part):
    tiles, size, width = raw.shape
    parts = tiles // part
    anywhere = pl.BlockSpec(memory_space=pl.ANY)
    place = pl.BlockSpec((part, size, size), lambda t, p: ((p[1] ^ 1) * parts + t, 0, 0))
    return pl.pallas_call(
        near_body,
        grid_spec=pltpu.PrefetchScalarGridSpec(
            num_scalar_prefetch=1,
            grid=(parts,),
            in_specs=[
                anywhere,
                anywhere,
                pl.BlockSpec((part, size, width), lambda t, p: (t, 0, 0)),
                whole(inverses_t),
                whole(couple_t),
                whole(keys_t),
                place,
            ],
            out_specs=place,
        ),
        out_shape=jax.ShapeDtypeStruct(trailing.shape, BF16),
        input_output_aliases={1: 0},
        compiler_params=pltpu.CompilerParams(vmem_limit_bytes=VMEM_LIMIT),
        cost_estimate=SMALL_COST,
    )(info, held, after, raw, inverses_t, couple_t, keys_t, trailing)


def gate(pieces, waited):
    anywhere = pl.BlockSpec(memory_space=pl.ANY)
    return pl.pallas_call(
        lambda *refs: None,
        in_specs=[anywhere] * (len(pieces) + len(waited)),
        out_specs=[anywhere] * len(pieces),
        out_shape=[jax.ShapeDtypeStruct(piece.shape, piece.dtype) for piece in pieces],
        input_output_aliases={i: i for i in range(len(pieces))},
        cost_estimate=SMALL_COST,
    )(*pieces, *waited)


def crossed_body(cols, info, after, raw, inverses_t, couple_t, keys_t, *pieces):
    del after
    part, size, width = raw.shape
    left, right = factor_rows(raw[...].reshape(part * size, width), inverses_t, couple_t[...])
    col = info[1]
    for k in range(cols // 2):
        target = jnp.clip(jnp.where(col < cols // 2, col - k, col + k), 0, cols - 1)
        total = times_key(left, right, keys_t[target])
        pieces[k][...] = total.reshape(part, size, size).astype(BF16)


def crossed_tiles(info, after, raw, first, count, inverses_t, couple_t, keys_t, part, cols):
    size, width = raw.shape[1:]
    skipped = first // part
    piece = jax.ShapeDtypeStruct((count, size, size), BF16)
    return pl.pallas_call(
        functools.partial(crossed_body, cols),
        grid_spec=pltpu.PrefetchScalarGridSpec(
            num_scalar_prefetch=1,
            grid=(count // part,),
            in_specs=[
                pl.BlockSpec(memory_space=pl.ANY),
                pl.BlockSpec((part, size, width), lambda t, p: (skipped + t, 0, 0)),
                whole(inverses_t),
                whole(couple_t),
                whole(keys_t),
            ],
            out_specs=[pl.BlockSpec((part, size, size), lambda t, p: (t, 0, 0))] * (cols // 2),
        ),
        out_shape=[piece] * (cols // 2),
        compiler_params=pltpu.CompilerParams(vmem_limit_bytes=VMEM_LIMIT),
        cost_estimate=SMALL_COST,
    )(info, after, raw, inverses_t, couple_t, keys_t)


def update_body(use_second, info, held, trailing, first, second, out):
    del held
    flag = use_second(info[1])

    @pl.when(jnp.logical_not(flag))
    def _():
        out[...] = (trailing[...].astype(jnp.float32) - first[...].astype(jnp.float32)).astype(BF16)

    @pl.when(flag)
    def _():
        out[...] = (trailing[...].astype(jnp.float32) - second[...].astype(jnp.float32)).astype(BF16)


def update(info, held, trailing, first, second, part, start, use_second):
    tiles, size, width = first.shape
    block = (part, size, width)
    place = pl.BlockSpec(block, lambda t, p: (start(p[1]) + t, 0, 0))
    return pl.pallas_call(
        functools.partial(update_body, use_second),
        grid_spec=pltpu.PrefetchScalarGridSpec(
            num_scalar_prefetch=1,
            grid=(tiles // part,),
            in_specs=[
                pl.BlockSpec(memory_space=pl.ANY),
                place,
                pl.BlockSpec(block, lambda t, p: (jnp.where(use_second(p[1]), 0, t), 0, 0)),
                pl.BlockSpec(block, lambda t, p: (jnp.where(use_second(p[1]), t, 0), 0, 0)),
            ],
            out_specs=place,
        ),
        out_shape=jax.ShapeDtypeStruct(trailing.shape, trailing.dtype),
        input_output_aliases={1: 0},
        compiler_params=pltpu.CompilerParams(vmem_limit_bytes=VMEM_LIMIT),
        cost_estimate=SMALL_COST,
    )(info, held, trailing, first, second)


def spread_heads(head, rows, cols):
    wanted = sorted({tile % rows for tile in range(1, cols + 2)})
    col_index = lax.axis_index("col")
    span = cols // 2
    while span:
        pairs = [
            (r * cols + c, r * cols + c + span) for r in wanted for c in range(0, cols, 2 * span)
        ]
        arrived = lax.ppermute(head, ("row", "col"), pairs)
        head = jnp.where(col_index % (2 * span) == span, arrived, head)
        span //= 2
    same = [head]
    for offset in range(2, rows, 2):
        same.append(lax.ppermute(head, "row", [(r, r ^ offset) for r in wanted]))
    same = jnp.stack(same)
    return same, lax.ppermute(same, "row", [(r, r ^ 1) for r in range(rows)])


def shards(panel_cols, inverses, trailing):
    tiles = panel_cols.shape[0]
    rows = lax.axis_size("row")
    cols = lax.axis_size("col")
    low, high = cols // 2 - 1, cols // 2
    part = 3 if tiles % 3 == 0 else 1
    halves = 2 if tiles % (2 * part) == 0 else 1
    half = tiles // halves
    info = jnp.stack([lax.axis_index("row"), lax.axis_index("col")]).astype(jnp.int32)
    inverses_t = jnp.swapaxes(inverses, 1, 2)

    crossed = lax.ppermute(panel_cols, "col", [(low, high), (high, low)])
    next_raw = lax.ppermute(panel_cols, "col", [(c, c ^ 1) for c in range(cols)])

    head_tiles = (cols + 1) // rows + 1
    same, other = spread_heads(panel_cols[:head_tiles], rows, cols)
    couple_t, keys_t = make_keys(info, same, other, inverses_t, rows, cols)
    small = (inverses_t, couple_t, keys_t)

    out, *far = own_tiles(info, panel_cols, *small, trailing, part, cols)
    far = gate(far, [crossed, next_raw])
    arrived = {}
    for offset in range(cols - 1, 1, -1):
        pairs = [
            (c, c ^ offset)
            for c in range(cols)
            if not (c == low and c ^ offset > low) and not (c == high and c ^ offset < high)
        ]
        arrived[offset] = lax.ppermute(far[offset - 2], "col", pairs)

    outward = []
    col_index = lax.axis_index("col")
    after = far[-1]
    for i in range(halves):
        mine, *handed = crossed_tiles(info, after, crossed, i * half, half, *small, part, cols)
        after = mine
        got = [
            lax.ppermute(handed[k], "col", [(high, high + k + 1), (low, low - k - 1)])
            for k in range(cols // 2 - 1)
        ]
        chosen = got[0]
        for k in range(1, len(got)):
            here = (col_index == high + k + 1) | (col_index == low - k - 1)
            chosen = jnp.where(here, got[k], chosen)
        outward.append((mine, chosen))

    out = near_tiles(info, out, after, next_raw, *small, trailing, part)

    for offset in range(2, cols - 1):
        def second(col, offset=offset):
            return (col ^ special_source(col, cols)) <= offset

        def source(col, offset=offset, second=second):
            return (col ^ jnp.where(second(col), offset + 1, offset)) * (tiles // part)

        out = update(
            info, out, trailing, arrived[offset], arrived[offset + 1], part, source, second
        )

    def outer(col):
        return (col != low) & (col != high)

    for i, (mine, got) in enumerate(outward):
        out = update(
            info, out, trailing, mine, got, part,
            lambda col, i=i: (special_source(col, cols) * tiles + i * half) // part, outer,
        )
    return out


def solution(mesh):
    in_specs = (P("col", "row", None), P(), P(None, "row", "col"))
    out_specs = P(None, "row", "col")
    return jax.shard_map(shards, mesh=mesh, in_specs=in_specs, out_specs=out_specs, check_vma=False)
```

```python
import functools

import jax
import jax.numpy as jnp
from jax import lax
from jax.experimental import pallas as pl
from jax.experimental.pallas import tpu as pltpu
from jax.sharding import PartitionSpec as P

BF16 = jnp.bfloat16
SMALL_COST = pl.CostEstimate(flops=1024, bytes_accessed=1024, transcendentals=0)


def vmem_limit():
    return (8 + 3 * lax.axis_size("col")) * 1024 * 1024


def dot(left, right):
    return jnp.dot(left, right, preferred_element_type=jnp.float32)


def factor_rows(rows, inverses_t, couple_t):
    size = couple_t.shape[0]
    left = dot(rows[:, :size], inverses_t[0]).astype(BF16)
    reduced = (rows[:, size:].astype(jnp.float32) - dot(left, couple_t)).astype(BF16)
    right = dot(reduced, inverses_t[1]).astype(BF16)
    return left, right


def times_key(left, right, key_t):
    size = left.shape[1]
    return dot(left, key_t[:size]) + dot(right, key_t[size:])


def special_source(col, cols):
    return cols // 2 - (col >= cols // 2)


def keys_body(rows, info, same, other, inverses_t, couple_t, keys_t):
    size = couple_t.shape[0]

    def raw(tile):
        offset = info[0] ^ (tile % rows)
        index, place = offset // 2, tile // rows
        return jnp.where(offset % 2 == 0, same[index, place], other[index, place])

    couple = dot(raw(1)[:, :size], inverses_t[0]).astype(BF16)
    couple_t[...] = couple.astype(jnp.float32).T.astype(BF16)
    for j in range(keys_t.shape[0]):
        left, right = factor_rows(raw(j + 2), inverses_t, couple_t[...])
        keys_t[j, :size] = left.astype(jnp.float32).T.astype(BF16)
        keys_t[j, size:] = right.astype(jnp.float32).T.astype(BF16)


def make_keys(info, same, other, inverses_t, rows, cols):
    size, width = same.shape[2:]
    vmem = pl.BlockSpec(memory_space=pltpu.VMEM)
    return pl.pallas_call(
        functools.partial(keys_body, rows),
        in_specs=[pl.BlockSpec(memory_space=pltpu.SMEM), vmem, vmem, vmem],
        out_specs=[vmem, vmem],
        out_shape=[
            jax.ShapeDtypeStruct((size, size), BF16),
            jax.ShapeDtypeStruct((cols, width, size), BF16),
        ],
        compiler_params=pltpu.CompilerParams(vmem_limit_bytes=vmem_limit()),
        cost_estimate=SMALL_COST,
    )(info, same, other, inverses_t)


def whole(array):
    return pl.BlockSpec(array.shape, lambda t, p: (0,) * array.ndim)


def own_body(info, panel, inverses_t, couple_t, keys_t, trailing, out, factored):
    part, size, width = panel.shape
    left, right = factor_rows(panel[...].reshape(part * size, width), inverses_t, couple_t[...])
    total = times_key(left, right, keys_t[info[1]]).reshape(part, size, size)
    out[...] = (trailing[...].astype(jnp.float32) - total).astype(BF16)
    factored[:, :, :size] = left.reshape(part, size, size)
    factored[:, :, size:] = right.reshape(part, size, size)


def own_tiles(info, panel, inverses_t, couple_t, keys_t, trailing, part):
    tiles, size, width = panel.shape
    parts = tiles // part
    rows = pl.BlockSpec((part, size, width), lambda t, p: (t, 0, 0))
    mine = pl.BlockSpec((part, size, size), lambda t, p: (p[1] * parts + t, 0, 0))
    return pl.pallas_call(
        own_body,
        grid_spec=pltpu.PrefetchScalarGridSpec(
            num_scalar_prefetch=1,
            grid=(parts,),
            in_specs=[rows, whole(inverses_t), whole(couple_t), whole(keys_t), mine],
            out_specs=[mine, rows],
        ),
        out_shape=[
            jax.ShapeDtypeStruct(trailing.shape, BF16),
            jax.ShapeDtypeStruct(panel.shape, BF16),
        ],
        compiler_params=pltpu.CompilerParams(vmem_limit_bytes=vmem_limit()),
        cost_estimate=SMALL_COST,
    )(info, panel, inverses_t, couple_t, keys_t, trailing)


def far_body(offset, info, after, factored, keys_t, piece):
    del after
    part, size, width = factored.shape
    rows = factored[...].reshape(part * size, width)
    total = dot(rows, keys_t[info[1] ^ offset])
    piece[...] = total.reshape(part, size, size).astype(BF16)


def far_product(info, after, factored, keys_t, offset, part):
    tiles, size, width = factored.shape
    return pl.pallas_call(
        functools.partial(far_body, offset),
        grid_spec=pltpu.PrefetchScalarGridSpec(
            num_scalar_prefetch=1,
            grid=(tiles // part,),
            in_specs=[
                pl.BlockSpec(memory_space=pl.ANY),
                pl.BlockSpec((part, size, width), lambda t, p: (t, 0, 0)),
                whole(keys_t),
            ],
            out_specs=pl.BlockSpec((part, size, size), lambda t, p: (t, 0, 0)),
        ),
        out_shape=jax.ShapeDtypeStruct((tiles, size, size), BF16),
        compiler_params=pltpu.CompilerParams(vmem_limit_bytes=vmem_limit()),
        cost_estimate=SMALL_COST,
    )(info, after, factored, keys_t)


def near_body(info, held, after, raw, inverses_t, couple_t, keys_t, trailing, out):
    del held, after
    part, size, width = raw.shape
    left, right = factor_rows(raw[...].reshape(part * size, width), inverses_t, couple_t[...])
    total = times_key(left, right, keys_t[info[1]]).reshape(part, size, size)
    out[...] = (trailing[...].astype(jnp.float32) - total).astype(BF16)


def near_tiles(info, held, after, raw, inverses_t, couple_t, keys_t, trailing, part):
    count, size, width = raw.shape
    parts = trailing.shape[0] // part // lax.axis_size("col")
    place = pl.BlockSpec((part, size, size), lambda t, p: ((p[1] ^ 1) * parts + t, 0, 0))
    return pl.pallas_call(
        near_body,
        grid_spec=pltpu.PrefetchScalarGridSpec(
            num_scalar_prefetch=1,
            grid=(count // part,),
            in_specs=[
                pl.BlockSpec(memory_space=pl.ANY),
                pl.BlockSpec(memory_space=pl.ANY),
                pl.BlockSpec((part, size, width), lambda t, p: (t, 0, 0)),
                whole(inverses_t),
                whole(couple_t),
                whole(keys_t),
                place,
            ],
            out_specs=place,
        ),
        out_shape=jax.ShapeDtypeStruct(trailing.shape, BF16),
        input_output_aliases={1: 0},
        compiler_params=pltpu.CompilerParams(vmem_limit_bytes=vmem_limit()),
        cost_estimate=SMALL_COST,
    )(info, held, after, raw, inverses_t, couple_t, keys_t, trailing)


def copy_after(panel, part, after):
    def body(after, tiles, out):
        del after
        out[...] = tiles[...]

    block = pl.BlockSpec((part,) + panel.shape[1:], lambda t: (t, 0, 0))
    return pl.pallas_call(
        body,
        grid=(panel.shape[0] // part,),
        in_specs=[pl.BlockSpec(memory_space=pl.ANY), block],
        out_specs=block,
        out_shape=jax.ShapeDtypeStruct(panel.shape, panel.dtype),
        compiler_params=pltpu.CompilerParams(vmem_limit_bytes=vmem_limit()),
        cost_estimate=SMALL_COST,
    )(after, panel)


def crossed_body(cols, info, after, raw, inverses_t, couple_t, keys_t, *pieces):
    del after
    part, size, width = raw.shape
    left, right = factor_rows(raw[...].reshape(part * size, width), inverses_t, couple_t[...])
    col = info[1]
    for k in range(cols // 2):
        target = jnp.clip(jnp.where(col < cols // 2, col - k, col + k), 0, cols - 1)
        total = times_key(left, right, keys_t[target])
        pieces[k][...] = total.reshape(part, size, size).astype(BF16)


def crossed_tiles(info, after, raw, first, count, inverses_t, couple_t, keys_t, part, cols):
    size, width = raw.shape[1:]
    skipped = first // part
    piece = jax.ShapeDtypeStruct((count, size, size), BF16)
    return pl.pallas_call(
        functools.partial(crossed_body, cols),
        grid_spec=pltpu.PrefetchScalarGridSpec(
            num_scalar_prefetch=1,
            grid=(count // part,),
            in_specs=[
                pl.BlockSpec(memory_space=pl.ANY),
                pl.BlockSpec((part, size, width), lambda t, p: (skipped + t, 0, 0)),
                whole(inverses_t),
                whole(couple_t),
                whole(keys_t),
            ],
            out_specs=[pl.BlockSpec((part, size, size), lambda t, p: (t, 0, 0))] * (cols // 2),
        ),
        out_shape=[piece] * (cols // 2),
        compiler_params=pltpu.CompilerParams(vmem_limit_bytes=vmem_limit()),
        cost_estimate=SMALL_COST,
    )(info, after, raw, inverses_t, couple_t, keys_t)


def update_body(which, info, held, trailing, *refs):
    del held
    *pieces, out = refs
    for i, piece in enumerate(pieces):
        @pl.when(which(info[1]) == i)
        def _(piece=piece):
            total = trailing[...].astype(jnp.float32) - piece[...].astype(jnp.float32)
            out[...] = total.astype(BF16)


def update(info, held, trailing, pieces, count, part, start, which):
    block = (part,) + trailing.shape[1:]
    place = pl.BlockSpec(block, lambda t, p: (start(p[1]) + t, 0, 0))

    def chosen(i, first):
        skipped = first // part
        return pl.BlockSpec(
            block, lambda t, p: (skipped + jnp.where(which(p[1]) == i, t, 0), 0, 0)
        )

    return pl.pallas_call(
        functools.partial(update_body, which),
        grid_spec=pltpu.PrefetchScalarGridSpec(
            num_scalar_prefetch=1,
            grid=(count // part,),
            in_specs=[pl.BlockSpec(memory_space=pl.ANY), place]
            + [chosen(i, first) for i, (_, first) in enumerate(pieces)],
            out_specs=place,
        ),
        out_shape=jax.ShapeDtypeStruct(trailing.shape, trailing.dtype),
        input_output_aliases={1: 0},
        compiler_params=pltpu.CompilerParams(vmem_limit_bytes=vmem_limit()),
        cost_estimate=SMALL_COST,
    )(info, held, trailing, *[array for array, _ in pieces])


def spread_down(head, wanted, cols):
    steps = []
    col_index = lax.axis_index("col")
    span = cols // 2
    while span:
        pairs = [
            (r * cols + c, r * cols + c + span) for r in wanted for c in range(0, cols, 2 * span)
        ]
        arrived = lax.ppermute(head, ("row", "col"), pairs)
        head = jnp.where(col_index % (2 * span) == span, arrived, head)
        steps.append(head)
        span //= 2
    return head, steps[0]


def spread_across(head, wanted, rows):
    same = [head]
    for offset in range(2, rows, 2):
        same.append(lax.ppermute(head, "row", [(r, r ^ offset) for r in wanted]))
    same = jnp.stack(same)
    return same, lax.ppermute(same, "row", [(r, r ^ 1) for r in range(rows)])


def shards(panel_cols, inverses, trailing):
    tiles = panel_cols.shape[0]
    rows = lax.axis_size("row")
    cols = lax.axis_size("col")
    low, high = cols // 2 - 1, cols // 2
    part = 3 if tiles % 3 == 0 else 1
    parts = tiles // part
    halves = 2 if parts % 2 == 0 else 1
    half = tiles // halves
    info = jnp.stack([lax.axis_index("row"), lax.axis_index("col")]).astype(jnp.int32)
    inverses_t = jnp.swapaxes(inverses, 1, 2)

    crossed = lax.ppermute(panel_cols, "col", [(low, high), (high, low)])

    wanted = sorted({tile % rows for tile in range(1, cols + 2)})
    head, first_step = spread_down(panel_cols[:(cols + 1) // rows + 1], wanted, cols)
    beside = [(c, c ^ 1) for c in range(cols)]
    next_raw = lax.ppermute(copy_after(panel_cols, part, first_step), "col", beside)
    same, other = spread_across(head, wanted, rows)
    couple_t, keys_t = make_keys(info, same, other, inverses_t, rows, cols)
    small = (inverses_t, couple_t, keys_t)

    out, factored = own_tiles(info, panel_cols, *small, trailing, part)
    arrived = {}
    after = out
    for offset in range(cols - 1, 1, -1):
        pairs = [
            (c, c ^ offset)
            for c in range(cols)
            if not (c == low and c ^ offset > low) and not (c == high and c ^ offset < high)
        ]
        after = far_product(info, after, factored, keys_t, offset, part)
        arrived[offset] = lax.ppermute(after, "col", pairs)

    outward = []
    col_index = lax.axis_index("col")
    for i in range(halves):
        mine, *handed = crossed_tiles(info, after, crossed, i * half, half, *small, part, cols)
        after = mine
        got = [
            lax.ppermute(handed[k], "col", [(high, high + k + 1), (low, low - k - 1)])
            for k in range(cols // 2 - 1)
        ]
        chosen = got[0]
        for k in range(1, len(got)):
            here = (col_index == high + k + 1) | (col_index == low - k - 1)
            chosen = jnp.where(here, got[k], chosen)
        outward.append((mine, chosen))

    out = near_tiles(info, out, after, next_raw, *small, trailing, part)

    def far_offset(col, slot):
        return slot + ((col ^ special_source(col, cols)) <= slot)

    def inner(col):
        return (col == low) | (col == high)

    for slot in range(3, cols - 1):
        out = update(
            info, out, trailing, [(arrived[slot], 0), (arrived[slot + 1], 0)], tiles, part,
            lambda col, slot=slot: (col ^ far_offset(col, slot)) * parts,
            lambda col, slot=slot: far_offset(col, slot) - slot,
        )

    outer_far = sorted({far_offset(c, 2) for c in range(cols) if not inner(c)})

    def far_place(col):
        return (col ^ far_offset(col, 2)) * parts

    for i, (mine, _) in enumerate(outward):
        out = update(
            info, out, trailing,
            [(mine, 0)] + [(arrived[offset], i * half) for offset in outer_far], half, part,
            lambda col, i=i: i * half // part
            + jnp.where(inner(col), special_source(col, cols) * parts, far_place(col)),
            lambda col: jnp.where(inner(col), 0, far_offset(col, 2) - outer_far[0] + 1),
        )
    for i, (_, got) in enumerate(outward):
        out = update(
            info, out, trailing, [(got, 0), (arrived[2], i * half)], half, part,
            lambda col, i=i: i * half // part
            + jnp.where(inner(col), far_place(col), special_source(col, cols) * parts),
            lambda col: jnp.where(inner(col), 1, 0),
        )
    return out


def solution(mesh):
    in_specs = (P("col", "row", None), P(), P(None, "row", "col"))
    out_specs = P(None, "row", "col")
    return jax.shard_map(shards, mesh=mesh, in_specs=in_specs, out_specs=out_specs, check_vma=False)
```

```python
import functools

import jax
import jax.numpy as jnp
from jax import lax
from jax.experimental import pallas as pl
from jax.experimental.pallas import tpu as pltpu
from jax.sharding import PartitionSpec as P

BF16 = jnp.bfloat16
SMALL_FLOPS, OWN_FLOPS = 1024, 5 * 10**9
ANYWHERE = pl.BlockSpec(memory_space=pl.ANY)


def call(body, grid, in_specs, out_specs, out_shape, held=False, flops=SMALL_FLOPS):
    return pl.pallas_call(
        body,
        grid_spec=pltpu.PrefetchScalarGridSpec(
            num_scalar_prefetch=1, grid=grid, in_specs=in_specs, out_specs=out_specs
        ),
        out_shape=out_shape,
        input_output_aliases={1: 0} if held else {},
        compiler_params=pltpu.CompilerParams(
            vmem_limit_bytes=(8 + 3 * lax.axis_size("col")) * 1024 * 1024
        ),
        cost_estimate=pl.CostEstimate(flops=flops, bytes_accessed=1024, transcendentals=0),
    )


def whole(array):
    return pl.BlockSpec(array.shape, lambda t, p: (0,) * array.ndim)


def tiles_at(array, count, start):
    shape = tuple(pl.Element(extent) for extent in (count,) + array.shape[1:])
    return pl.BlockSpec(shape, lambda t, p: (start(t, p[1]), 0, 0))


def step_of(count):
    return max(step for step in range(1, 6) if count % step == 0)


def shape_of(count, size, width=None):
    return jax.ShapeDtypeStruct((count, size, width or size), BF16)


def dot(left, right):
    return jnp.dot(left, right, preferred_element_type=jnp.float32)


def factor_rows(rows, inverses_t, couple_t):
    size = couple_t.shape[0]
    left = dot(rows[:, :size], inverses_t[0]).astype(BF16)
    reduced = (rows[:, size:].astype(jnp.float32) - dot(left, couple_t)).astype(BF16)
    right = dot(reduced, inverses_t[1]).astype(BF16)
    return left, right


def factor_tiles(tiles, inverses_t, couple_t):
    count, size, width = tiles.shape
    return factor_rows(tiles[...].reshape(count * size, width), inverses_t, couple_t[...])


def times_key(left, right, key_t):
    size = left.shape[1]
    total = dot(left, key_t[:size]) + dot(right, key_t[size:])
    return total.reshape(-1, size, size)


def subtract(trailing, total):
    return (trailing[...].astype(jnp.float32) - total).astype(BF16)


def keys_body(rows, info, same, other, inverses_t, couple_t, keys_t):
    size = couple_t.shape[0]

    def raw(tile):
        offset = info[0] ^ (tile % rows)
        index, place = offset // 2, tile // rows
        return jnp.where(offset % 2 == 0, same[index, place], other[index, place])

    couple = dot(raw(1)[:, :size], inverses_t[0]).astype(BF16)
    couple_t[...] = couple.astype(jnp.float32).T.astype(BF16)
    for j in range(keys_t.shape[0]):
        left, right = factor_rows(raw(j + 2), inverses_t, couple_t[...])
        keys_t[j, :size] = left.astype(jnp.float32).T.astype(BF16)
        keys_t[j, size:] = right.astype(jnp.float32).T.astype(BF16)


def make_keys(info, same, other, inverses_t, rows, cols):
    size, width = same.shape[2:]
    couple_t = jax.ShapeDtypeStruct((size, size), BF16)
    keys_t = jax.ShapeDtypeStruct((cols, width, size), BF16)
    return call(
        functools.partial(keys_body, rows),
        (1,),
        [whole(same), whole(other), whole(inverses_t)],
        [whole(couple_t), whole(keys_t)],
        [couple_t, keys_t],
    )(info, same, other, inverses_t)


def own_body(info, panel, inverses_t, couple_t, keys_t, trailing, out, factored):
    left, right = factor_tiles(panel, inverses_t, couple_t)
    out[...] = subtract(trailing, times_key(left, right, keys_t[info[1]]))
    count, size = panel.shape[:2]
    factored[:, :, :size] = left.reshape(count, size, size)
    factored[:, :, size:] = right.reshape(count, size, size)


def own_tiles(info, panel, small, trailing):
    tiles = panel.shape[0]
    step = step_of(tiles)
    rows = tiles_at(panel, step, lambda t, col: t * step)
    mine = tiles_at(trailing, step, lambda t, col: col * tiles + t * step)
    return call(
        own_body,
        (tiles // step,),
        [rows, *map(whole, small), mine],
        [mine, rows],
        [
            jax.ShapeDtypeStruct(trailing.shape, BF16),
            jax.ShapeDtypeStruct(panel.shape, BF16),
        ],
        flops=OWN_FLOPS,
    )(info, panel, *small, trailing)


def products_body(offset, first, info, after, factored, keys_t, piece):
    del after
    tiles, size, width = factored.shape
    key_t = keys_t[info[1] ^ offset]
    middle = first + (tiles - first) // 2
    for start, stop in ((first, middle), (middle, tiles)):
        rows = factored[start:stop].reshape((stop - start) * size, width)
        total = dot(rows, key_t).reshape(stop - start, size, size)
        piece[start - first:stop - first] = total.astype(BF16)


def products(info, after, factored, keys_t, offset, first):
    tiles, size, _ = factored.shape
    piece = shape_of(tiles - first, size)
    return call(
        functools.partial(products_body, offset, first),
        (1,),
        [ANYWHERE, whole(factored), whole(keys_t)],
        whole(piece),
        piece,
    )(info, after, factored, keys_t)


def raw_body(info, held, after, raw, inverses_t, couple_t, keys_t, trailing, out):
    del held, after
    left, right = factor_tiles(raw, inverses_t, couple_t)
    out[...] = subtract(trailing, times_key(left, right, keys_t[info[1]]))


def raw_tiles(info, held, after, raw, small, trailing, place):
    count = raw.shape[0]
    step = step_of(count)
    spot = tiles_at(trailing, step, lambda t, col: place(col) + t * step)
    return call(
        raw_body,
        (count // step,),
        [
            ANYWHERE,
            ANYWHERE,
            tiles_at(raw, step, lambda t, col: t * step),
            *map(whole, small),
            spot,
        ],
        spot,
        jax.ShapeDtypeStruct(trailing.shape, BF16),
        held=True,
    )(info, held, after, raw, *small, trailing)


def crossed_body(cols, info, after, raw, inverses_t, couple_t, keys_t, *pieces):
    del after
    left, right = factor_tiles(raw, inverses_t, couple_t)
    col = info[1]
    for k in range(cols // 2):
        target = jnp.clip(jnp.where(col < cols // 2, col - k, col + k), 0, cols - 1)
        pieces[k][...] = times_key(left, right, keys_t[target]).astype(BF16)


def crossed_tiles(info, after, raw, first, count, small, cols):
    step = step_of(count)
    piece = shape_of(count, raw.shape[1])
    return call(
        functools.partial(crossed_body, cols),
        (count // step,),
        [ANYWHERE, tiles_at(raw, step, lambda t, col: first + t * step), *map(whole, small)],
        [tiles_at(piece, step, lambda t, col: t * step)] * (cols // 2),
        [piece] * (cols // 2),
    )(info, after, raw, *small)


def update_body(which, info, held, trailing, *refs):
    del held
    *pieces, out = refs
    for i, piece in enumerate(pieces):
        @pl.when(which(info[1]) == i)
        def _(piece=piece):
            out[...] = subtract(trailing, piece[...].astype(jnp.float32))


def update(info, held, trailing, count, pieces, which):
    step = step_of(count)

    def place(col):
        spot = pieces[0][2](col)
        for i, (_, _, start) in enumerate(pieces[1:], 1):
            spot = jnp.where(which(col) == i, start(col), spot)
        return spot

    def chosen(i, array, first):
        return tiles_at(
            array, step, lambda t, col: first + jnp.where(which(col) == i, t * step, 0)
        )

    spot = tiles_at(trailing, step, lambda t, col: place(col) + t * step)
    return call(
        functools.partial(update_body, which),
        (count // step,),
        [ANYWHERE, spot] + [chosen(i, array, first) for i, (array, first, _) in enumerate(pieces)],
        spot,
        jax.ShapeDtypeStruct(trailing.shape, BF16),
        held=True,
    )(info, held, trailing, *[array for array, _, _ in pieces])


def copy_after(panel, first, waited):
    count, size, width = panel.shape[0] - first, *panel.shape[1:]
    step = step_of(count)

    def body(*refs):
        *_, tiles, out = refs
        out[...] = tiles[...]

    shape = shape_of(count, size, width)
    return call(
        body,
        (count // step,),
        [ANYWHERE] * len(waited) + [tiles_at(panel, step, lambda t, col: first + t * step)],
        tiles_at(shape, step, lambda t, col: t * step),
        shape,
    )(jnp.zeros((2,), jnp.int32), *waited, panel)


def spread_ends(first, cols):
    col = lax.axis_index("col")
    kept = first
    span = cols // 2
    while span > 1:
        pairs = []
        for c in range(0, cols, 2 * span):
            pairs += [(c, c + span), (cols - 1 - c, cols - 1 - c - span)]
        arrived = lax.ppermute(kept, "col", pairs)
        reached = (col % (2 * span) == span) | ((cols - 1 - col) % (2 * span) == span)
        kept = jnp.where(reached, arrived, kept)
        span //= 2
    return kept


def spread_across(head, wanted, rows):
    same = [head]
    for offset in range(2, rows, 2):
        same.append(lax.ppermute(head, "row", [(r, r ^ offset) for r in wanted]))
    same = jnp.stack(same)
    return same, lax.ppermute(same, "row", [(r, r ^ 1) for r in range(rows)])


def special_source(col, cols):
    return cols // 2 - (col >= cols // 2)


def shards(panel_cols, inverses, trailing):
    tiles = panel_cols.shape[0]
    rows = lax.axis_size("row")
    cols = lax.axis_size("col")
    col_index = lax.axis_index("col")
    low, high = cols // 2 - 1, cols // 2
    info = jnp.stack([lax.axis_index("row"), col_index]).astype(jnp.int32)
    inverses_t = jnp.swapaxes(inverses, 1, 2)

    head_tiles = (cols + 1) // rows + 1
    beside = [(c, c ^ 1) for c in range(cols)]
    inside = [(c, c ^ 1) for c in range(1, cols - 1)]

    crossed = lax.ppermute(panel_cols, "col", [(low, high), (high, low)])
    kept = spread_ends(panel_cols[:head_tiles], cols)
    near_first = lax.ppermute(panel_cols[:head_tiles], "col", beside)
    passed = lax.ppermute(kept, "col", inside)
    near_last = lax.ppermute(copy_after(panel_cols, head_tiles, [kept, near_first]), "col", beside)
    from_end = (col_index == 1) | (col_index == cols - 2)
    passed = jnp.where(from_end, near_first, passed)
    even = col_index % 2 == 0
    head = jnp.where(even, kept, passed)

    wanted = sorted({tile % rows for tile in range(1, cols + 2)})
    same, other = spread_across(head, wanted, rows)
    couple_t, keys_t = make_keys(info, same, other, inverses_t, rows, cols)
    small = (inverses_t, couple_t, keys_t)
    out, factored = own_tiles(info, panel_cols, small, trailing)

    sends = {
        offset: [
            (c, c ^ offset)
            for c in range(cols)
            if not (c == low and c ^ offset > low) and not (c == high and c ^ offset < high)
        ]
        for offset in range(cols - 1, 1, -1)
    }
    ends_only = all(c in (0, cols - 1) for pairs in sends.values() for c, _ in pairs)
    skipped = head_tiles if ends_only else 0
    arrived = {}
    after = out
    for offset, pairs in sends.items():
        after = products(info, after, factored, keys_t, offset, skipped)
        arrived[offset] = lax.ppermute(after, "col", pairs)

    out = raw_tiles(
        info, out, after, near_last, small, trailing, lambda col: (col ^ 1) * tiles + head_tiles
    )
    half = tiles // 2 if tiles % 2 == 0 else tiles
    mine, got = [], []
    after = out
    for first in range(0, tiles, half):
        after, *handed = crossed_tiles(info, after, crossed, first, half, small, cols)
        mine.append(after)
        handed = [
            lax.ppermute(piece, "col", [(high, high + k), (low, low - k)])
            for k, piece in enumerate(handed, 1)
        ]
        got.append(handed[0])
        for k, piece in enumerate(handed[1:], 2):
            here = (col_index == high + k) | (col_index == low - k)
            got[-1] = jnp.where(here, piece, got[-1])

    out = raw_tiles(info, out, after, near_first, small, trailing, lambda col: (col ^ 1) * tiles)
    if ends_only:
        far_head = jnp.where((col_index <= low) == even, passed, kept)
        out = raw_tiles(
            info, out, after, far_head, small, trailing,
            lambda col: jnp.where(col <= low, (cols - 1) * tiles, 0),
        )

    def far_offset(col, slot=2):
        return slot + ((col ^ special_source(col, cols)) <= slot)

    def inner(col):
        return (col == low) | (col == high)

    def special(array, i):
        return array, 0, lambda col: special_source(col, cols) * tiles + i * half

    def far(offset, i):
        first = min(i * half, tiles - skipped - half)
        return arrived[offset], first, lambda col: (col ^ offset) * tiles + skipped + first

    for slot in range(3, cols - 1):
        for i in range(tiles // half):
            out = update(
                info, out, trailing, half, [far(slot, i), far(slot + 1, i)],
                lambda col, slot=slot: far_offset(col, slot) - slot,
            )
    outer_far = sorted({far_offset(c) for c in range(cols) if not inner(c)})
    for i in range(tiles // half):
        out = update(
            info, out, trailing, half,
            [special(mine[i], i)] + [far(offset, i) for offset in outer_far],
            lambda col: jnp.where(inner(col), 0, far_offset(col) - outer_far[0] + 1),
        )
    for i in range(tiles // half):
        out = update(
            info, out, trailing, half, [special(got[i], i), far(2, i)],
            lambda col: jnp.where(inner(col), 1, 0),
        )
    return out


def solution(mesh):
    in_specs = (P("col", "row", None), P(), P(None, "row", "col"))
    out_specs = P(None, "row", "col")
    return jax.shard_map(shards, mesh=mesh, in_specs=in_specs, out_specs=out_specs, check_vma=False)
```

```python
import functools

import jax
import jax.numpy as jnp
from jax import lax
from jax.experimental import pallas as pl
from jax.experimental.pallas import tpu as pltpu
from jax.sharding import PartitionSpec as P

BF16 = jnp.bfloat16
SMALL_FLOPS, OWN_FLOPS = 1024, 5 * 10**9
ANYWHERE = pl.BlockSpec(memory_space=pl.ANY)


def call(body, grid, in_specs, out_specs, out_shape, held=False, flops=SMALL_FLOPS):
    return pl.pallas_call(
        body,
        grid_spec=pltpu.PrefetchScalarGridSpec(
            num_scalar_prefetch=1, grid=grid, in_specs=in_specs, out_specs=out_specs
        ),
        out_shape=out_shape,
        input_output_aliases={1: 0} if held else {},
        compiler_params=pltpu.CompilerParams(
            vmem_limit_bytes=(8 + 3 * lax.axis_size("col")) * 1024 * 1024
        ),
        cost_estimate=pl.CostEstimate(flops=flops, bytes_accessed=1024, transcendentals=0),
    )


def whole(array):
    return pl.BlockSpec(array.shape, lambda t, p: (0,) * array.ndim)


def tiles_at(array, count, start):
    shape = tuple(pl.Element(extent) for extent in (count,) + array.shape[1:])
    return pl.BlockSpec(shape, lambda t, p: (start(t, p[1]), 0, 0))


def steps_of(count):
    steps = -(-count // 4)
    step = -(-count // steps)
    if count % step == 0:
        return step, steps, lambda t: t * step
    return step, steps, lambda t: jnp.minimum(t * step, count - step)


def shape_of(count, size, width=None):
    return jax.ShapeDtypeStruct((count, size, width or size), BF16)


def dot(left, right):
    return jnp.dot(left, right, preferred_element_type=jnp.float32)


def factor_rows(rows, inverses_t, couple_t):
    size = couple_t.shape[0]
    left = dot(rows[:, :size], inverses_t[0]).astype(BF16)
    reduced = (rows[:, size:].astype(jnp.float32) - dot(left, couple_t)).astype(BF16)
    right = dot(reduced, inverses_t[1]).astype(BF16)
    return left, right


def factor_tiles(tiles, inverses_t, couple_t):
    count, size, width = tiles.shape
    return factor_rows(tiles[...].reshape(count * size, width), inverses_t, couple_t[...])


def times_key(left, right, key_t):
    size = left.shape[1]
    total = dot(left, key_t[:size]) + dot(right, key_t[size:])
    return total.reshape(-1, size, size)


def subtract(trailing, total):
    return (trailing[...].astype(jnp.float32) - total).astype(BF16)


def keys_body(rows, info, same, other, inverses_t, couple_t, keys_t):
    size = couple_t.shape[0]

    def raw(tile):
        offset = info[0] ^ (tile % rows)
        index, place = offset // 2, tile // rows
        return jnp.where(offset % 2 == 0, same[index, place], other[index, place])

    couple = dot(raw(1)[:, :size], inverses_t[0]).astype(BF16)
    couple_t[...] = couple.astype(jnp.float32).T.astype(BF16)
    for j in range(keys_t.shape[0]):
        left, right = factor_rows(raw(j + 2), inverses_t, couple_t[...])
        keys_t[j, :size] = left.astype(jnp.float32).T.astype(BF16)
        keys_t[j, size:] = right.astype(jnp.float32).T.astype(BF16)


def make_keys(info, same, other, inverses_t, rows, cols):
    size, width = same.shape[2:]
    couple_t = jax.ShapeDtypeStruct((size, size), BF16)
    keys_t = jax.ShapeDtypeStruct((cols, width, size), BF16)
    return call(
        functools.partial(keys_body, rows),
        (1,),
        [whole(same), whole(other), whole(inverses_t)],
        [whole(couple_t), whole(keys_t)],
        [couple_t, keys_t],
    )(info, same, other, inverses_t)


def own_body(info, panel, inverses_t, couple_t, keys_t, trailing, out, factored):
    left, right = factor_tiles(panel, inverses_t, couple_t)
    out[...] = subtract(trailing, times_key(left, right, keys_t[info[1]]))
    count, size = panel.shape[:2]
    factored[:, :, :size] = left.reshape(count, size, size)
    factored[:, :, size:] = right.reshape(count, size, size)


def own_tiles(info, panel, small, trailing):
    tiles = panel.shape[0]
    step, steps, at = steps_of(tiles)
    rows = tiles_at(panel, step, lambda t, col: at(t))
    mine = tiles_at(trailing, step, lambda t, col: col * tiles + at(t))
    return call(
        own_body,
        (steps,),
        [rows, *map(whole, small), mine],
        [mine, rows],
        [
            jax.ShapeDtypeStruct(trailing.shape, BF16),
            jax.ShapeDtypeStruct(panel.shape, BF16),
        ],
        flops=OWN_FLOPS,
    )(info, panel, *small, trailing)


def products_body(offset, first, info, after, factored, keys_t, piece):
    del after
    tiles, size, width = factored.shape
    key_t = keys_t[info[1] ^ offset]
    middle = first + (tiles - first) // 2
    for start, stop in ((first, middle), (middle, tiles)):
        rows = factored[start:stop].reshape((stop - start) * size, width)
        total = dot(rows, key_t).reshape(stop - start, size, size)
        piece[start - first:stop - first] = total.astype(BF16)


def products(info, after, factored, keys_t, offset, first):
    tiles, size, _ = factored.shape
    piece = shape_of(tiles - first, size)
    return call(
        functools.partial(products_body, offset, first),
        (1,),
        [ANYWHERE, whole(factored), whole(keys_t)],
        whole(piece),
        piece,
    )(info, after, factored, keys_t)


def raw_body(info, held, after, raw, inverses_t, couple_t, keys_t, trailing, out, done):
    del held, after
    done[...] = jnp.zeros_like(done)
    left, right = factor_tiles(raw, inverses_t, couple_t)
    out[...] = subtract(trailing, times_key(left, right, keys_t[info[1]]))


def raw_tiles(info, held, after, raw, small, trailing, place):
    count = raw.shape[0]
    step, steps, at = steps_of(count)
    spot = tiles_at(trailing, step, lambda t, col: place(col) + at(t))
    done = jax.ShapeDtypeStruct((8, 128), jnp.float32)
    return call(
        raw_body,
        (steps,),
        [
            ANYWHERE,
            ANYWHERE,
            tiles_at(raw, step, lambda t, col: at(t)),
            *map(whole, small),
            spot,
        ],
        [spot, whole(done)],
        [jax.ShapeDtypeStruct(trailing.shape, BF16), done],
        held=True,
    )(info, held, after, raw, *small, trailing)


def crossed_body(cols, info, after, raw, inverses_t, couple_t, keys_t, *pieces):
    del after
    left, right = factor_tiles(raw, inverses_t, couple_t)
    col = info[1]
    for k in range(cols // 2):
        target = jnp.clip(jnp.where(col < cols // 2, col - k, col + k), 0, cols - 1)
        pieces[k][...] = times_key(left, right, keys_t[target]).astype(BF16)


def crossed_tiles(info, after, raw, first, count, small, cols):
    step, steps, at = steps_of(count)
    piece = shape_of(count, raw.shape[1])
    return call(
        functools.partial(crossed_body, cols),
        (steps,),
        [ANYWHERE, tiles_at(raw, step, lambda t, col: first + at(t)), *map(whole, small)],
        [tiles_at(piece, step, lambda t, col: at(t))] * (cols // 2),
        [piece] * (cols // 2),
    )(info, after, raw, *small)


def update_body(which, info, held, trailing, *refs):
    del held
    *pieces, out = refs
    for i, piece in enumerate(pieces):
        @pl.when(which(info[1]) == i)
        def _(piece=piece):
            out[...] = subtract(trailing, piece[...].astype(jnp.float32))


def update(info, held, trailing, count, pieces, which):
    step, steps, at = steps_of(count)

    def place(col):
        spot = pieces[0][2](col)
        for i, (_, _, start) in enumerate(pieces[1:], 1):
            spot = jnp.where(which(col) == i, start(col), spot)
        return spot

    def chosen(i, array, first):
        return tiles_at(
            array, step, lambda t, col: first + jnp.where(which(col) == i, at(t), 0)
        )

    spot = tiles_at(trailing, step, lambda t, col: place(col) + at(t))
    return call(
        functools.partial(update_body, which),
        (steps,),
        [ANYWHERE, spot] + [chosen(i, array, first) for i, (array, first, _) in enumerate(pieces)],
        spot,
        jax.ShapeDtypeStruct(trailing.shape, BF16),
        held=True,
    )(info, held, trailing, *[array for array, _, _ in pieces])


def gate(array, waited):
    return call(
        lambda *refs: None,
        (1,),
        [ANYWHERE] * (1 + len(waited)),
        ANYWHERE,
        jax.ShapeDtypeStruct(array.shape, array.dtype),
        held=True,
    )(jnp.zeros((2,), jnp.int32), array, *waited)


def spread_ends(first, cols):
    col = lax.axis_index("col")
    kept = first
    span = cols // 2
    while span > 1:
        pairs = []
        for c in range(0, cols, 2 * span):
            pairs += [(c, c + span), (cols - 1 - c, cols - 1 - c - span)]
        arrived = lax.ppermute(kept, "col", pairs)
        reached = (col % (2 * span) == span) | ((cols - 1 - col) % (2 * span) == span)
        kept = jnp.where(reached, arrived, kept)
        span //= 2
    return kept


def spread_across(head, wanted, rows):
    same = [head]
    for offset in range(2, rows, 2):
        same.append(lax.ppermute(head, "row", [(r, r ^ offset) for r in wanted]))
    same = jnp.stack(same)
    return same, lax.ppermute(same, "row", [(r, r ^ 1) for r in range(rows)])


def special_source(col, cols):
    return cols // 2 - (col >= cols // 2)


def shards(panel_cols, inverses, trailing):
    tiles = panel_cols.shape[0]
    rows = lax.axis_size("row")
    cols = lax.axis_size("col")
    col_index = lax.axis_index("col")
    low, high = cols // 2 - 1, cols // 2
    info = jnp.stack([lax.axis_index("row"), col_index]).astype(jnp.int32)
    inverses_t = jnp.swapaxes(inverses, 1, 2)

    head_tiles = (cols + 1) // rows + 1
    beside = [(c, c ^ 1) for c in range(cols)]
    inside = [(c, c ^ 1) for c in range(1, cols - 1)]

    crossed = lax.ppermute(panel_cols, "col", [(low, high), (high, low)])
    kept = spread_ends(panel_cols[:head_tiles], cols)
    near_first = lax.ppermute(panel_cols[:head_tiles], "col", beside)
    rest = panel_cols[head_tiles:]
    kept = gate(kept, [rest])
    passed = lax.ppermute(kept, "col", inside)
    near_last = lax.ppermute(gate(rest, [kept, near_first]), "col", beside)
    from_end = (col_index == 1) | (col_index == cols - 2)
    passed = jnp.where(from_end, near_first, passed)
    even = col_index % 2 == 0
    head = jnp.where(even, kept, passed)

    wanted = sorted({tile % rows for tile in range(1, cols + 2)})
    same, other = spread_across(head, wanted, rows)
    couple_t, keys_t = make_keys(info, same, other, inverses_t, rows, cols)
    small = (inverses_t, couple_t, keys_t)
    out, factored = own_tiles(info, panel_cols, small, trailing)

    sends = {
        offset: [
            (c, c ^ offset)
            for c in range(cols)
            if not (c == low and c ^ offset > low) and not (c == high and c ^ offset < high)
        ]
        for offset in range(cols - 1, 1, -1)
    }
    ends_only = all(c in (0, cols - 1) for pairs in sends.values() for c, _ in pairs)
    skipped = head_tiles if ends_only else 0
    arrived = {}
    after = factored
    for offset, pairs in sends.items():
        after = products(info, after, factored, keys_t, offset, skipped)
        arrived[offset] = lax.ppermute(after, "col", pairs)

    out, after = raw_tiles(
        info, out, after, near_last, small, trailing, lambda col: (col ^ 1) * tiles + head_tiles
    )
    half = tiles // 2 if tiles % 2 == 0 else tiles
    mine, got = [], []
    for first in range(0, tiles, half):
        after, *handed = crossed_tiles(info, after, crossed, first, half, small, cols)
        mine.append(after)
        handed = [
            lax.ppermute(piece, "col", [(high, high + k), (low, low - k)])
            for k, piece in enumerate(handed, 1)
        ]
        got.append(handed[0])
        for k, piece in enumerate(handed[1:], 2):
            here = (col_index == high + k) | (col_index == low - k)
            got[-1] = jnp.where(here, piece, got[-1])

    out, after = raw_tiles(
        info, out, after, near_first, small, trailing, lambda col: (col ^ 1) * tiles
    )
    if ends_only:
        far_head = jnp.where((col_index <= low) == even, passed, kept)
        out, after = raw_tiles(
            info, out, after, far_head, small, trailing,
            lambda col: jnp.where(col <= low, (cols - 1) * tiles, 0),
        )

    def far_offset(col, slot=2):
        return slot + ((col ^ special_source(col, cols)) <= slot)

    def inner(col):
        return (col == low) | (col == high)

    def special(array, i):
        return array, 0, lambda col: special_source(col, cols) * tiles + i * half

    def far(offset, i):
        first = min(i * half, tiles - skipped - half)
        return arrived[offset], first, lambda col: (col ^ offset) * tiles + skipped + first

    for slot in range(3, cols - 1):
        for i in range(tiles // half):
            out = update(
                info, out, trailing, half, [far(slot, i), far(slot + 1, i)],
                lambda col, slot=slot: far_offset(col, slot) - slot,
            )
    outer_far = sorted({far_offset(c) for c in range(cols) if not inner(c)})
    for i in range(tiles // half):
        out = update(
            info, out, trailing, half,
            [special(mine[i], i)] + [far(offset, i) for offset in outer_far],
            lambda col: jnp.where(inner(col), 0, far_offset(col) - outer_far[0] + 1),
        )
    for i in range(tiles // half):
        out = update(
            info, out, trailing, half, [special(got[i], i), far(2, i)],
            lambda col: jnp.where(inner(col), 1, 0),
        )
    return out


def solution(mesh):
    in_specs = (P("col", "row", None), P(), P(None, "row", "col"))
    out_specs = P(None, "row", "col")
    return jax.shard_map(shards, mesh=mesh, in_specs=in_specs, out_specs=out_specs, check_vma=False)
```

```python
import functools

import jax
import jax.numpy as jnp
from jax import lax
from jax.experimental import pallas as pl
from jax.experimental.pallas import tpu as pltpu
from jax.sharding import PartitionSpec as P

BF16 = jnp.bfloat16
COST = {"own": 2, "keys": 2, "products": 0, "tail": 1, "raw": 5, "crossed": 1, "update": 1, "gate": 0}
ANYWHERE = pl.BlockSpec(memory_space=pl.ANY)


def call(kind, body, grid, in_specs, out_specs, out_shape, held=False):
    return pl.pallas_call(
        body,
        grid_spec=pltpu.PrefetchScalarGridSpec(
            num_scalar_prefetch=1, grid=grid, in_specs=in_specs, out_specs=out_specs
        ),
        out_shape=out_shape,
        input_output_aliases={1: 0} if held else {},
        compiler_params=pltpu.CompilerParams(
            vmem_limit_bytes=(8 + 3 * lax.axis_size("col")) * 1024 * 1024
        ),
        cost_estimate=pl.CostEstimate(
            flops=1024 + int(COST[kind] * 1e9), bytes_accessed=1024, transcendentals=0
        ),
    )


def whole(array):
    return pl.BlockSpec(array.shape, lambda t, p: (0,) * array.ndim)


def tiles_at(array, count, start):
    shape = tuple(pl.Element(extent) for extent in (count,) + array.shape[1:])
    return pl.BlockSpec(shape, lambda t, p: (start(t, p[1]), 0, 0))


def steps_of(count):
    steps = -(-count // 4)
    step = -(-count // steps)
    if count % step == 0:
        return step, steps, lambda t: t * step
    return step, steps, lambda t: jnp.minimum(t * step, count - step)


def shape_of(count, size, width=None):
    return jax.ShapeDtypeStruct((count, size, width or size), BF16)


def dot(left, right):
    return jnp.dot(left, right, preferred_element_type=jnp.float32)


def factor_rows(rows, inverses_t, couple_t):
    size = couple_t.shape[0]
    left = dot(rows[:, :size], inverses_t[0]).astype(BF16)
    reduced = (rows[:, size:].astype(jnp.float32) - dot(left, couple_t)).astype(BF16)
    right = dot(reduced, inverses_t[1]).astype(BF16)
    return left, right


def factor_tiles(tiles, inverses_t, couple_t):
    count, size, width = tiles.shape
    return factor_rows(tiles[...].reshape(count * size, width), inverses_t, couple_t[...])


def times_key(left, right, key_t):
    size = left.shape[1]
    total = dot(left, key_t[:size]) + dot(right, key_t[size:])
    return total.reshape(-1, size, size)


def subtract(trailing, total):
    return (trailing[...].astype(jnp.float32) - total).astype(BF16)


def keys_body(rows, info, same, other, inverses_t, couple_t, keys_t):
    size = couple_t.shape[0]

    def raw(tile):
        offset = info[0] ^ (tile % rows)
        index, place = offset // 2, tile // rows
        return jnp.where(offset % 2 == 0, same[index, place], other[index, place])

    couple = dot(raw(1)[:, :size], inverses_t[0]).astype(BF16)
    couple_t[...] = couple.astype(jnp.float32).T.astype(BF16)
    for j in range(keys_t.shape[0]):
        left, right = factor_rows(raw(j + 2), inverses_t, couple_t[...])
        keys_t[j, :size] = left.astype(jnp.float32).T.astype(BF16)
        keys_t[j, size:] = right.astype(jnp.float32).T.astype(BF16)


def make_keys(info, same, other, inverses_t, rows, cols):
    size, width = same.shape[2:]
    couple_t = jax.ShapeDtypeStruct((size, size), BF16)
    keys_t = jax.ShapeDtypeStruct((cols, width, size), BF16)
    return call(
        "keys",
        functools.partial(keys_body, rows),
        (1,),
        [whole(same), whole(other), whole(inverses_t)],
        [whole(couple_t), whole(keys_t)],
        [couple_t, keys_t],
    )(info, same, other, inverses_t)


def own_body(info, panel, inverses_t, couple_t, keys_t, trailing, out, factored):
    left, right = factor_tiles(panel, inverses_t, couple_t)
    out[...] = subtract(trailing, times_key(left, right, keys_t[info[1]]))
    count, size = panel.shape[:2]
    factored[:, :, :size] = left.reshape(count, size, size)
    factored[:, :, size:] = right.reshape(count, size, size)


def own_tiles(info, panel, small, trailing):
    tiles = panel.shape[0]
    step, steps, at = steps_of(tiles)
    rows = tiles_at(panel, step, lambda t, col: at(t))
    mine = tiles_at(trailing, step, lambda t, col: col * tiles + at(t))
    return call(
        "own",
        own_body,
        (steps,),
        [rows, *map(whole, small), mine],
        [mine, rows],
        [
            jax.ShapeDtypeStruct(trailing.shape, BF16),
            jax.ShapeDtypeStruct(panel.shape, BF16),
        ],
    )(info, panel, *small, trailing)


def products_body(offset, first, info, after, factored, keys_t, piece, *last):
    del after
    tiles, size, width = factored.shape
    key_t = keys_t[info[1] ^ offset]
    middle = first + (tiles - first) // 2
    for start, stop in ((first, middle), (middle, tiles)):
        rows = factored[start:stop].reshape((stop - start) * size, width)
        total = dot(rows, key_t).reshape(stop - start, size, size)
        piece[start - first:stop - first] = total.astype(BF16)
    for array in last:
        array[...] = piece[tiles - first - array.shape[0]:]


def products(info, after, factored, keys_t, offset, first, last=0):
    tiles, size, _ = factored.shape
    shapes = [shape_of(count, size) for count in (tiles - first, last) if count]
    return call(
        "products",
        functools.partial(products_body, offset, first),
        (1,),
        [ANYWHERE, whole(factored), whole(keys_t)],
        [whole(shape) for shape in shapes],
        shapes,
    )(info, after, factored, keys_t)


def tail_body(offset, info, factored, keys_t, piece):
    count, size, width = factored.shape
    total = dot(factored[...].reshape(count * size, width), keys_t[info[1] ^ offset(info[1])])
    piece[...] = total.reshape(count, size, size).astype(BF16)


def tail_products(info, factored, keys_t, count, offset):
    tiles, size, _ = factored.shape
    piece = shape_of(count, size)
    return call(
        "tail",
        functools.partial(tail_body, offset),
        (1,),
        [tiles_at(factored, count, lambda t, col: tiles - count), whole(keys_t)],
        whole(piece),
        piece,
    )(info, factored, keys_t)


def raw_body(info, held, after, raw, inverses_t, couple_t, keys_t, trailing, out, done):
    del held, after
    done[...] = jnp.zeros_like(done)
    left, right = factor_tiles(raw, inverses_t, couple_t)
    out[...] = subtract(trailing, times_key(left, right, keys_t[info[1]]))


def raw_tiles(info, held, after, raw, small, trailing, place):
    count = raw.shape[0]
    step, steps, at = steps_of(count)
    spot = tiles_at(trailing, step, lambda t, col: place(col) + at(t))
    done = jax.ShapeDtypeStruct((8, 128), jnp.float32)
    return call(
        "raw",
        raw_body,
        (steps,),
        [
            ANYWHERE,
            ANYWHERE,
            tiles_at(raw, step, lambda t, col: at(t)),
            *map(whole, small),
            spot,
        ],
        [spot, whole(done)],
        [jax.ShapeDtypeStruct(trailing.shape, BF16), done],
        held=True,
    )(info, held, after, raw, *small, trailing)


def crossed_body(cols, at, own, info, after, raw, factored, inverses_t, couple_t, keys_t, *pieces):
    del after
    count, size, width = raw.shape
    left, right = factor_tiles(raw, inverses_t, couple_t)
    place = pl.ds(at(pl.program_id(0)), count)
    col = info[1]
    for k, piece in enumerate(pieces):
        target = jnp.clip(jnp.where(col < cols // 2, col - k, col + k), 0, cols - 1)
        piece[place] = times_key(left, right, keys_t[target]).astype(BF16)
    if own:
        @pl.when(pl.program_id(0) == 0)
        def _():
            total = dot(factored[...].reshape(own * size, width), keys_t[col ^ 1])
            pieces[1][pieces[1].shape[0] - own:] = total.reshape(own, size, size).astype(BF16)


def crossed_tiles(info, after, raw, factored, own, small, cols):
    count, size, _ = raw.shape
    step, steps, at = steps_of(count)
    tail = tiles_at(factored, max(own, 1), lambda t, col: factored.shape[0] - max(own, 1))
    pieces = [shape_of(count + own * (k == 1), size) for k in range(cols // 2)]
    return call(
        "crossed",
        functools.partial(crossed_body, cols, at, own),
        (steps,),
        [ANYWHERE, tiles_at(raw, step, lambda t, col: at(t)), tail, *map(whole, small)],
        [whole(piece) for piece in pieces],
        pieces,
    )(info, after, raw, factored, *small)


def update_body(which, info, held, trailing, *refs):
    del held
    *pieces, out = refs
    for i, piece in enumerate(pieces):
        @pl.when(which(info[1]) == i)
        def _(piece=piece):
            out[...] = subtract(trailing, piece[...].astype(jnp.float32))


def update(info, held, trailing, count, pieces, which, step=None):
    if step is None:
        step, steps, at = steps_of(count)
    else:
        steps, at = count // step, lambda t: t * step

    def place(t, col):
        spot = pieces[0][2](col, at(t))
        for i, (_, _, start) in enumerate(pieces[1:], 1):
            spot = jnp.where(which(col) == i, start(col, at(t)), spot)
        return spot

    def chosen(i, array, first):
        return tiles_at(
            array, step, lambda t, col: first + jnp.where(which(col) == i, at(t), 0)
        )

    spot = tiles_at(trailing, step, place)
    return call(
        "update",
        functools.partial(update_body, which),
        (steps,),
        [ANYWHERE, spot] + [chosen(i, array, first) for i, (array, first, _) in enumerate(pieces)],
        spot,
        jax.ShapeDtypeStruct(trailing.shape, BF16),
        held=True,
    )(info, held, trailing, *[array for array, _, _ in pieces])


def gate(array, waited):
    return call(
        "gate",
        lambda *refs: None,
        (1,),
        [ANYWHERE] * (1 + len(waited)),
        ANYWHERE,
        jax.ShapeDtypeStruct(array.shape, array.dtype),
        held=True,
    )(jnp.zeros((2,), jnp.int32), array, *waited)


def spread_ends(first, cols):
    col = lax.axis_index("col")
    kept = first
    span = cols // 2
    while span > 1:
        pairs = []
        for c in range(0, cols, 2 * span):
            pairs += [(c, c + span), (cols - 1 - c, cols - 1 - c - span)]
        arrived = lax.ppermute(kept, "col", pairs)
        reached = (col % (2 * span) == span) | ((cols - 1 - col) % (2 * span) == span)
        kept = jnp.where(reached, arrived, kept)
        span //= 2
    return kept


def spread_across(head, wanted, rows):
    same = [head]
    for offset in range(2, rows, 2):
        same.append(lax.ppermute(head, "row", [(r, r ^ offset) for r in wanted]))
    same = jnp.stack(same)
    return same, lax.ppermute(same, "row", [(r, r ^ 1) for r in range(rows)])


def special_source(col, cols):
    return cols // 2 - (col >= cols // 2)


def shards(panel_cols, inverses, trailing):
    tiles = panel_cols.shape[0]
    rows = lax.axis_size("row")
    cols = lax.axis_size("col")
    col_index = lax.axis_index("col")
    low, high = cols // 2 - 1, cols // 2
    info = jnp.stack([lax.axis_index("row"), col_index]).astype(jnp.int32)
    inverses_t = jnp.swapaxes(inverses, 1, 2)
    swap = [(low, high), (high, low)]
    beside = [(c, c ^ 1) for c in range(cols)]
    inside = beside[1:-1]

    sends = {
        offset: [
            (c, c ^ offset)
            for c in range(cols)
            if not (c == low and c ^ offset > low) and not (c == high and c ^ offset < high)
        ]
        for offset in range(cols - 1, 1, -1)
    }
    ends_only = all(c in (0, cols - 1) for pairs in sends.values() for c, _ in pairs)
    head_tiles = (cols + 1) // rows + 1
    skipped = head_tiles if ends_only else 0
    half = tiles // 2 if tiles % 2 == 0 else tiles
    direct = 2 if ends_only and half > 3 else 0
    last = tiles - direct

    crossed = lax.ppermute(panel_cols[:last], "col", swap)
    kept = spread_ends(panel_cols[:head_tiles], cols)
    near_first = lax.ppermute(panel_cols[:head_tiles], "col", beside)
    rest = panel_cols[head_tiles:last]
    kept = gate(kept, [rest])
    passed = lax.ppermute(kept, "col", inside)
    near_rest = lax.ppermute(gate(rest, [kept, near_first]), "col", beside)
    from_end = (col_index == 1) | (col_index == cols - 2)
    passed = jnp.where(from_end, near_first, passed)
    even = col_index % 2 == 0
    head = jnp.where(even, kept, passed)

    wanted = sorted({tile % rows for tile in range(1, cols + 2)})
    same, other = spread_across(head, wanted, rows)
    couple_t, keys_t = make_keys(info, same, other, inverses_t, rows, cols)
    small = (inverses_t, couple_t, keys_t)
    out, factored = own_tiles(info, panel_cols, small, trailing)

    def inner(col):
        return (col == low) | (col == high)

    after = factored
    if direct:
        after = tail_products(
            info, factored, keys_t, direct, lambda col: jnp.where(inner(col), 2, 1)
        )
        last_round = lax.ppermute(after, "col", [(0, 1), (1, 3), (3, 2), (2, 0)])
    arrived = {}
    for offset, pairs in sends.items():
        straight = direct if offset == high ^ low else 0
        after, *last_swap = products(info, after, factored, keys_t, offset, skipped, straight)
        arrived[offset] = lax.ppermute(after, "col", pairs)
        if straight:
            last_crossed = lax.ppermute(last_swap[0], "col", swap)

    after, *handed = crossed_tiles(info, after, crossed, factored, direct, small, cols)
    mine = after
    handed = [
        lax.ppermute(piece, "col", [(high, high + k), (low, low - k)])
        for k, piece in enumerate(handed, 1)
    ]
    got = handed[0]
    for k, piece in enumerate(handed[1:], 2):
        got = jnp.where((col_index == high + k) | (col_index == low - k), piece, got)

    out, after = raw_tiles(
        info, out, after, near_rest, small, trailing, lambda col: (col ^ 1) * tiles + head_tiles
    )
    out, after = raw_tiles(
        info, out, after, near_first, small, trailing, lambda col: (col ^ 1) * tiles
    )
    if ends_only:
        far_head = jnp.where((col_index <= low) == even, passed, kept)
        out, after = raw_tiles(
            info, out, after, far_head, small, trailing,
            lambda col: jnp.where(col <= low, (cols - 1) * tiles, 0),
        )

    def far_offset(col, slot=2):
        return slot + ((col ^ special_source(col, cols)) <= slot)

    def special(array, i):
        start = min(i * half, array.shape[0] - half)
        return array, start, lambda col, tile: (
            special_source(col, cols) * tiles + start + tile
        )

    def far(offset, i):
        start = min(i * half, tiles - skipped - half)
        return arrived[offset], start, lambda col, tile: (
            (col ^ offset) * tiles + skipped + start + tile
        )

    for slot in range(3, cols - 1):
        for i in range(tiles // half):
            out = update(
                info, out, trailing, half, [far(slot, i), far(slot + 1, i)],
                lambda col, slot=slot: far_offset(col, slot) - slot,
            )
    outer_far = sorted({far_offset(c) for c in range(cols) if not inner(c)})
    for i in range(tiles // half):
        out = update(
            info, out, trailing, half,
            [special(mine, i)] + [far(offset, i) for offset in outer_far],
            lambda col: jnp.where(inner(col), 0, far_offset(col) - outer_far[0] + 1),
        )
    if direct:
        def round_place(col, tile):
            return jnp.where(inner(col), col ^ 1, special_source(col, cols)) * tiles + last + tile

        out = update(info, out, trailing, direct, [(last_round, 0, round_place)], lambda col: 0)
        crossed_place = lambda col, tile: special_source(col, cols) * tiles + last + tile
        out = update(
            info, out, trailing, direct,
            [(last_crossed, 0, crossed_place), (last_round, 0, round_place)],
            lambda col: jnp.where(inner(col), 0, 1),
        )
    for i in range(tiles // half):
        array, start, usual = special(got, i)

        def place(col, tile, start=start, usual=usual):
            return jnp.where(start + tile < last, usual(col, tile), (col ^ 1) * tiles + start + tile)

        out = update(
            info, out, trailing, half, [(array, start, place), far(2, i)],
            lambda col: jnp.where(inner(col), 1, 0), direct if i else None,
        )
    return out


def solution(mesh):
    in_specs = (P("col", "row", None), P(), P(None, "row", "col"))
    out_specs = P(None, "row", "col")
    return jax.shard_map(shards, mesh=mesh, in_specs=in_specs, out_specs=out_specs, check_vma=False)
```
